32 devices in a mesh: island: 2 (over y), stripe: 4 (over z), rep: 4 (over x, core).
Axes of the slice: x: 2, y: 2, z: 4, core: 2. Of those that a mesh axis runs over, the one named last changes fastest.
Arguments:
- features: bfloat16 [4096, 256], P(('island', 'stripe', 'rep')), parts along dimension 0, may hold values from -6 to 6
- tiles: bfloat16 [8, 4, 3, 128, 128], P(('island', 'stripe'), 'rep'), parts along dimension 0, as said below
- tile_row: int32 [8, 4, 3], P(('island', 'stripe'), 'rep'), parts along dimension 0, may hold values from 0 to 4, as said below
- tile_src: int32 [8, 4, 3], P(('island', 'stripe'), 'rep'), parts along dimension 0, may hold values from 0 to 3, as said below
- self_weight: bfloat16 [256, 256], replicated, may hold values from -0.375 to 0.375
- neigh_weight: bfloat16 [256, 256], replicated, may hold values from -4 to 4
- bias: bfloat16 [256], replicated, may hold values from -3 to 3
- cotangent: bfloat16 [4096, 256], P(('island', 'stripe', 'rep')), parts along dimension 0, may hold values from -6 to 6
Outputs:
- output: bfloat16 [4096, 256], P(('island', 'stripe', 'rep')), parts along dimension 0
- grad_input: float32 [4096, 256], P(('island', 'stripe', 'rep')), parts along dimension 0
- grad_self: float32 [512, 256], P('island'), parts along dimension 0
- grad_neigh: float32 [512, 256], P('island'), parts along dimension 0
- grad_bias: float32 [512], P('island'), parts along dimension 0
The draws below stay inside these ranges and needn't reach their ends.
There are 2 independent parts, one for each index of `island`. The reference program is written for one: setup_inputs(seed, part) draws one part's arguments, and reference() takes and returns one part's arrays. A program takes and returns all parts, laid end to end along the dimension named above; an argument that names none is the same for every part. Nothing has to cross between parts.
Inputs may be any that keep to these rules, and one draw needn't show every extreme that they name: `tiles`: Non-negative edge weights; within a tile the nonzero share and the row scales vary. `tile_row`: value 4 marks an unused slot. Each device has a live slot for its own stripe and one for one other stripe, and for every destination stripe one device has a live slot for the stripe 4 // 2 away; all other slots are unused. A node has some 30 neighbours on average. `tile_src`: the source stripe of a slot; live slots as described for tile_row.
All inputs are finite; a program needn't handle non-finite values.
Results may differ from the reference program's by a relative error of at most 0.019.
Values may be sent and summed in bfloat16 or wider, within the bound.
A program may use at most 64 MiB of HBM per device.

```python
import math
import jax
import jax.numpy as jnp
from jax import lax

FEAT = 256
HID = 256
TILE = 128
K = 3
NODES = 2048
N_STRIPE = 4
N_REP = 4


def slot_layout(key):
    key_other, key_far, key_shift, key_block, key_spare = jax.random.split(key, 5)
    shape = (N_STRIPE, N_REP, K)
    dest = jnp.arange(N_STRIPE, dtype=jnp.int32)[:, None, None]
    reps = jnp.arange(N_REP, dtype=jnp.int32)[None, :, None]
    slot = jnp.arange(K, dtype=jnp.int32)[None, None, :]
    offset = jax.random.randint(key_other, (N_STRIPE, N_REP, 1), 1, N_STRIPE, jnp.int32)
    other = (dest + offset) % N_STRIPE
    far_rep = jax.random.randint(key_far, (N_STRIPE, 1, 1), 0, N_REP, jnp.int32)
    far_source = (dest + N_STRIPE // 2) % N_STRIPE
    shift = jax.random.randint(key_shift, (N_STRIPE, N_REP, 1), 0, K, jnp.int32)
    role = (slot - shift + K) % K
    spare = jax.random.randint(key_spare, shape, 0, N_STRIPE, jnp.int32)
    src = jnp.where(role == 0, dest, jnp.where(role == 1, other, jnp.where(role == 2, far_source, spare)))
    live = (role == 0) | (role == 1) | (role == 2) & (reps == far_rep)
    block = jax.random.randint(key_block, shape, 0, N_REP, jnp.int32)
    row = jnp.where(live, block, N_REP)
    return (row.astype(jnp.int32), src.astype(jnp.int32))


def draw_tiles(key, part):
    key = jax.random.fold_in(key, 11)
    key_share, key_keep, key_scale, key_value = jax.random.split(key, 4)
    shape = (N_STRIPE, N_REP, K, TILE, TILE)
    share = jnp.exp(jax.random.uniform(key_share, (N_STRIPE, N_REP, K, 1, 1), jnp.float32, math.log(0.04), math.log(0.25)))
    keep = jax.random.uniform(key_keep, shape, jnp.float32) < share
    scale = jnp.exp(jax.random.uniform(key_scale, (N_STRIPE, N_REP, K, TILE, 1), jnp.float32, 0.0, math.log(10.0)))
    value = jax.random.uniform(key_value, shape, jnp.float32, 0.5, 1.5)
    return jnp.where(keep, value * scale, 0.0).astype(jnp.bfloat16)


def draw_tile_row(key, part):
    row, src = slot_layout(key)
    return row


def draw_tile_src(key, part):
    row, src = slot_layout(key)
    return src


def levels(rng, dims, pieces, low, high):
    def one(axis_at, blocks):
        draws = jax.random.uniform(jax.random.fold_in(jax.random.fold_in(rng, 6), axis_at), (blocks,), jnp.float32, low / len(pieces), high / len(pieces))
        return jnp.repeat(jnp.exp(draws), dims[axis_at] // blocks).reshape((-1,) + (1,) * (len(dims) - axis_at - 1))

    loudness = one(*pieces[0])
    for cut in pieces[1:]:
        loudness = loudness * one(*cut)
    return loudness


def centred(key, extent, scale, bound, cuts=(), kind=jnp.bfloat16):
    entries = jax.random.normal(key, extent, jnp.float32) * scale
    if len(cuts) > 0:
        entries = levels(key, extent, cuts, -0.22, 0.18) * entries
    return jnp.clip(entries, min=-bound, max=bound).astype(kind)


def setup_inputs(seed: int = 0, part: int = 0) -> dict:
    streams_of = jax.random.split(jax.random.key(seed), 9)
    part_splits = jax.random.split(jax.random.fold_in(streams_of[8], part), 9)
    features = centred(part_splits[0], (NODES, FEAT), 1.0, 6.0, ((0, 16),))
    tiles = draw_tiles(jax.random.fold_in(jax.random.fold_in(streams_of[8], part), 71), part)
    tile_row = draw_tile_row(jax.random.fold_in(jax.random.fold_in(streams_of[8], part), 71), part)
    tile_src = draw_tile_src(jax.random.fold_in(jax.random.fold_in(streams_of[8], part), 71), part)
    self_weight = centred(streams_of[4], (FEAT, HID), FEAT ** -0.5, 0.375)
    neigh_weight = centred(streams_of[5], (FEAT, HID), (12.0 / FEAT ** 0.5), 4.0)
    bias = centred(streams_of[6], (HID,), 0.5, 3.0)
    cotangent = centred(part_splits[7], (NODES, HID), 1.0, 6.0, ((0, 16),))
    return dict(features=features, tiles=tiles, tile_row=tile_row, tile_src=tile_src, self_weight=self_weight, neigh_weight=neigh_weight, bias=bias, cotangent=cotangent)


def reference(features, tiles, tile_row, tile_src, self_weight, neigh_weight, bias, cotangent):
    high = lax.Precision.HIGHEST
    source = features.reshape(N_STRIPE, N_REP, TILE, FEAT).astype(jnp.float32)
    block_ids = jnp.arange(N_REP, dtype=jnp.int32)
    stripe_ids = jnp.arange(N_STRIPE, dtype=jnp.int32)
    rep_ids = jnp.arange(N_REP, dtype=jnp.int32)[:, None]

    def forward_stripe(inputs):
        tile_s, row_s, src_s = inputs
        onehot = (row_s[..., None] == block_ids).astype(jnp.float32)
        tile_f = tile_s.astype(jnp.float32)
        blocks = source[src_s, rep_ids]
        prod = jnp.einsum("rkab,rkbf->rkaf", tile_f, blocks, precision=high)
        agg = jnp.einsum("rkq,rkaf->qaf", onehot, prod, precision=high)
        sums = jnp.sum(tile_f, axis=-1)
        deg = 1.0 + jnp.einsum("rkq,rka->qa", onehot, sums, precision=high)
        return agg, deg

    aggregate, degree = lax.map(forward_stripe, (tiles, tile_row, tile_src))
    aggregate = aggregate.reshape(NODES, FEAT)
    degree = degree.reshape(NODES)
    neigh = (aggregate / degree[:, None]).astype(jnp.bfloat16)
    pre = (jnp.dot(features, self_weight, preferred_element_type=jnp.float32)
           + jnp.dot(neigh, neigh_weight, preferred_element_type=jnp.float32)
           + bias.astype(jnp.float32))
    output = jax.nn.silu(pre).astype(jnp.bfloat16)
    sigma = jax.nn.sigmoid(pre)
    slope = (cotangent.astype(jnp.float32) * sigma * (1.0 + pre * (1.0 - sigma))).astype(jnp.bfloat16)
    grad_self = jnp.dot(features.T, slope, preferred_element_type=jnp.float32)
    grad_neigh = jnp.dot(neigh.T, slope, preferred_element_type=jnp.float32)
    grad_bias = jnp.sum(slope.astype(jnp.float32), axis=0)
    pull = (jnp.dot(slope, neigh_weight.T, preferred_element_type=jnp.float32) / degree[:, None]).astype(jnp.bfloat16)
    pull_rows = pull.reshape(N_STRIPE, N_REP, TILE, FEAT).astype(jnp.float32)

    def backward_stripe(total, inputs):
        tile_s, row_s, src_s, pull_s = inputs
        onehot = (row_s[..., None] == block_ids).astype(jnp.float32)
        place = (src_s[..., None] == stripe_ids).astype(jnp.float32)
        picked = jnp.einsum("rkq,qaf->rkaf", onehot, pull_s, precision=high)
        slot_term = jnp.einsum("rkab,rkaf->rkbf", tile_s.astype(jnp.float32), picked, precision=high)
        term = jnp.einsum("rkt,rkbf->trbf", place, slot_term, precision=high)
        return total + term.astype(jnp.bfloat16).astype(jnp.float32), None

    start = jnp.zeros((N_STRIPE, N_REP, TILE, FEAT), jnp.float32)
    spread, _ = lax.scan(backward_stripe, start, (tiles, tile_row, tile_src, pull_rows))
    grad_input = jnp.dot(slope, self_weight.T, preferred_element_type=jnp.float32) + spread.reshape(NODES, FEAT)
    return output, grad_input, grad_self, grad_neigh, grad_bias
```

```python
import functools

import jax
import jax.numpy as jnp
from jax import lax
from jax.experimental import pallas as pl
from jax.experimental.pallas import tpu as pltpu
from jax.sharding import PartitionSpec as P

MESH = pl.DeviceIdType.MESH
BF16 = jnp.bfloat16
F32 = jnp.float32
PAD = 16


def matmul(a, b):
    return jnp.dot(a, b, preferred_element_type=F32)


def matmul_t(a, b):
    return lax.dot_general(a, b, (((1,), (1,)), ((), ())), preferred_element_type=F32)


def send(src, dst, sems, slot, device):
    return pltpu.make_async_remote_copy(
        src_ref=src,
        dst_ref=dst,
        send_sem=sems[0].at[slot],
        recv_sem=sems[1].at[slot],
        device_id=device,
        device_id_type=MESH,
    )


def kernel(
    stripes, reps, sub,
    row_ref, src_ref, feat_ref, tiles_ref, self_ref, neigh_ref, bias_ref, cot_ref,
    out_ref, gin_ref, gself_ref, gneigh_ref, gbias_ref,
    feat_buf, deg_send, deg_buf, agg_send, agg_buf, pull_buf, term_send, term_buf,
    rep_send, rep_buf, str_send, str_buf, all_str, all_rep, adj, adj_t,
    feat_s, feat_r, deg_s, deg_r, agg_s, agg_r, pull_s, pull_r, term_s, term_r,
    rep_s, rep_r, str_s, str_r, gst_s, gst_r, grp_s, grp_r,
):
    island = lax.axis_index("island")
    s = lax.axis_index("stripe")
    r = lax.axis_index("rep")
    edge, width = feat_ref.shape
    slots = tiles_ref.shape[2]

    def to_stripe(d):
        return (island, lax.rem(s + d, stripes), r)

    def to_rep(e):
        return (island, s, lax.rem(r + e, reps))

    barrier = pltpu.get_barrier_semaphore()
    for d in range(1, stripes):
        pl.semaphore_signal(barrier, inc=1, device_id=to_stripe(d), device_id_type=MESH)
    for e in range(1, reps):
        pl.semaphore_signal(barrier, inc=1, device_id=to_rep(e), device_id_type=MESH)
    pl.semaphore_wait(barrier, stripes + reps - 2)

    feat_copies = [
        send(feat_ref, feat_buf.at[d], (feat_s, feat_r), d, to_stripe(d)) for d in range(1, stripes)
    ]
    for copy in feat_copies:
        copy.start()

    tile = [tiles_ref[0, 0, k] for k in range(slots)]
    row = [row_ref[0, 0, k] for k in range(slots)]
    src = [src_ref[0, 0, k] for k in range(slots)]
    ones = jnp.ones((edge, edge), BF16)
    sums = [matmul(t, ones) for t in tile]
    for e in range(reps):
        q = lax.rem(r + e, reps)
        total = jnp.zeros((edge, edge), F32)
        for k in range(slots):
            total = total + jnp.where(row[k] == q, sums[k], 0.0)
        deg_send[e] = total.astype(BF16)
    deg_copies = [
        send(deg_send.at[e], deg_buf.at[e], (deg_s, deg_r), e, to_rep(e)) for e in range(1, reps)
    ]
    for copy in deg_copies:
        copy.start()

    zero = jnp.zeros((edge, edge), F32)
    tile_f = [t.astype(F32) for t in tile]
    tile_tf = [t.T for t in tile_f]

    def place(ref, e, d, values, q, t):
        total = zero
        for k in range(slots):
            total = total + jnp.where((row[k] == q) & (src[k] == t), values[k], 0.0)
        ref[e * edge:(e + 1) * edge, d * edge:(d + 1) * edge] = total.astype(BF16)

    for d in range(stripes):
        for e in range(reps):
            place(adj, e, d, tile_f, lax.rem(r + e, reps), lax.rem(s + stripes - d, stripes))
    for d in range(stripes):
        for e in range(reps):
            place(adj_t, d, e, tile_tf, lax.rem(r + reps - e, reps), lax.rem(s + d, stripes))

    feats = feat_ref[...]
    feats_t = feats.astype(F32).T.astype(BF16)
    pre_self = matmul(feats, self_ref[...]) + bias_ref[...].astype(F32)

    feat_buf[0] = feats
    for copy in feat_copies:
        copy.wait_recv()
    feat_all = feat_buf[...].reshape(stripes * edge, width)
    agg_copies = []
    for e in range(1, reps):
        agg_send[e] = matmul(adj[e * edge:(e + 1) * edge, :], feat_all).astype(BF16)
        copy = send(agg_send.at[e], agg_buf.at[e], (agg_s, agg_r), e, to_rep(e))
        copy.start()
        agg_copies.append(copy)
    agg = matmul(adj[0:edge, :], feat_all)
    degree = 1.0 + deg_send[0].astype(F32)
    for copy in deg_copies:
        copy.wait_recv()
    for e in range(1, reps):
        degree = degree + deg_buf[e].astype(F32)
    inverse = jnp.concatenate([1.0 / degree] * (width // edge), axis=1)
    for copy in agg_copies:
        copy.wait_recv()
    for e in range(1, reps):
        agg = agg + agg_buf[e].astype(F32)
    neigh = (agg * inverse).astype(BF16)

    pre = pre_self + matmul(neigh, neigh_ref[...])
    sigma = jax.nn.sigmoid(pre)
    slope = (cot_ref[...].astype(F32) * sigma * (1.0 + pre * (1.0 - sigma))).astype(BF16)

    pull_buf[0] = (matmul_t(slope, neigh_ref[...]) * inverse).astype(BF16)
    pull_copies = [
        send(pull_buf.at[0], pull_buf.at[e], (pull_s, pull_r), e, to_rep(e)) for e in range(1, reps)
    ]
    for copy in pull_copies:
        copy.start()

    chunk = rep_send.shape[1] - PAD
    neigh_t = neigh.astype(F32).T.astype(BF16)
    grad_bias = jnp.sum(slope.astype(F32), axis=0, keepdims=True)
    bias_rows = jnp.broadcast_to(grad_bias, (PAD, width)).astype(BF16)
    grads = jnp.concatenate([matmul(feats_t, slope), matmul(neigh_t, slope)], axis=0).astype(BF16)
    for c in range(reps):
        rep_send[c, :chunk] = grads[c * chunk:(c + 1) * chunk]
        rep_send[c, chunk:] = bias_rows
    rep_copies = [
        send(
            rep_send.at[lax.rem(r + e, reps)], rep_buf.at[e], (rep_s, rep_r), e, to_rep(e)
        )
        for e in range(1, reps)
    ]
    for copy in rep_copies:
        copy.start()
    out_ref[...] = (pre * sigma).astype(BF16)

    for copy in pull_copies:
        copy.wait_recv()
    pull_all = pull_buf[...].reshape(reps * edge, width)
    term_copies = []
    for d in range(1, stripes):
        term_send[d] = matmul(adj_t[d * edge:(d + 1) * edge, :], pull_all).astype(BF16)
        copy = send(term_send.at[d], term_buf.at[d], (term_s, term_r), d, to_stripe(d))
        copy.start()
        term_copies.append(copy)
    grad_input = matmul_t(slope, self_ref[...])
    grad_input = grad_input + matmul(adj_t[0:edge, :], pull_all).astype(BF16).astype(F32)

    share = rep_send[r].astype(F32)
    for copy in rep_copies:
        copy.wait_recv()
    for e in range(1, reps):
        share = share + rep_buf[e].astype(F32)
    if sub:
        share_b = share.astype(BF16)
        for c in range(stripes):
            str_send[c, :sub] = share_b[c * sub:(c + 1) * sub]
            str_send[c, sub:] = share_b[chunk:]
        str_copies = [
            send(
                str_send.at[lax.rem(s + d, stripes)], str_buf.at[d], (str_s, str_r), d, to_stripe(d)
            )
            for d in range(1, stripes)
        ]
        for copy in str_copies:
            copy.start()
        part = str_send[s].astype(F32)
        for copy in str_copies:
            copy.wait_recv()
        for d in range(1, stripes):
            part = part + str_buf[d].astype(F32)
        gbias_ref[...] = part[sub:sub + 1]
        all_str[s] = part[:sub].astype(BF16)
        gst_copies = [
            send(all_str.at[s], all_str.at[s], (gst_s, gst_r), d, to_stripe(d))
            for d in range(1, stripes)
        ]
        for copy in gst_copies:
            copy.start()
        for copy in gst_copies:
            copy.wait_recv()
        all_rep[r] = all_str[...].reshape(chunk, width)
    else:
        str_send[0] = share.astype(BF16)
        str_copies = [
            send(str_send.at[0], str_buf.at[d], (str_s, str_r), d, to_stripe(d))
            for d in range(1, stripes)
        ]
        for copy in str_copies:
            copy.start()
        part = share
        for copy in str_copies:
            copy.wait_recv()
        for d in range(1, stripes):
            part = part + str_buf[d].astype(F32)
        gbias_ref[...] = part[chunk:chunk + 1]
        all_rep[r] = part[:chunk].astype(BF16)
        gst_copies = []
    grp_copies = [
        send(all_rep.at[r], all_rep.at[r], (grp_s, grp_r), e, to_rep(e)) for e in range(1, reps)
    ]
    for copy in grp_copies:
        copy.start()

    for copy in term_copies:
        copy.wait_recv()
    for d in range(1, stripes):
        grad_input = grad_input + term_buf[d].astype(F32)
    gin_ref[...] = grad_input

    for copy in grp_copies:
        copy.wait_recv()
    half = reps // 2
    gself_ref[...] = all_rep[:half].reshape(half * chunk, width).astype(F32)
    gneigh_ref[...] = all_rep[half:].reshape(half * chunk, width).astype(F32)

    for copies in (
        feat_copies, deg_copies, agg_copies, pull_copies, rep_copies,
        term_copies, str_copies, gst_copies, grp_copies,
    ):
        for copy in copies:
            copy.wait_send()


def shards(features, tiles, tile_row, tile_src, self_weight, neigh_weight, bias, cotangent):
    stripes = lax.axis_size("stripe")
    reps = lax.axis_size("rep")
    edge, width = features.shape
    chunk = 2 * self_weight.shape[0] // reps
    sub = chunk // stripes if chunk % (PAD * stripes) == 0 else 0
    share = (stripes, sub + PAD, width) if sub else (stripes, chunk + PAD, width)
    vmem = pl.BlockSpec(memory_space=pltpu.VMEM)
    smem = pl.BlockSpec(memory_space=pltpu.SMEM)
    dma = pltpu.SemaphoreType.DMA
    by_rep = [dma((reps,)), dma((reps,))]
    by_stripe = [dma((stripes,)), dma((stripes,))]
    output, grad_input, grad_self, grad_neigh, grad_bias = pl.pallas_call(
        functools.partial(kernel, stripes, reps, sub),
        out_shape=(
            jax.ShapeDtypeStruct((edge, width), BF16),
            jax.ShapeDtypeStruct((edge, width), F32),
            jax.ShapeDtypeStruct(self_weight.shape, F32),
            jax.ShapeDtypeStruct(neigh_weight.shape, F32),
            jax.ShapeDtypeStruct((1, width), F32),
        ),
        in_specs=[smem, smem] + [vmem] * 6,
        out_specs=(vmem,) * 5,
        scratch_shapes=[
            pltpu.VMEM((stripes, edge, width), BF16),
            pltpu.VMEM((reps, edge, edge), BF16),
            pltpu.VMEM((reps, edge, edge), BF16),
            pltpu.VMEM((reps, edge, width), BF16),
            pltpu.VMEM((reps, edge, width), BF16),
            pltpu.VMEM((reps, edge, width), BF16),
            pltpu.VMEM((stripes, edge, width), BF16),
            pltpu.VMEM((stripes, edge, width), BF16),
            pltpu.VMEM((reps, chunk + PAD, width), BF16),
            pltpu.VMEM((reps, chunk + PAD, width), BF16),
            pltpu.VMEM(share, BF16),
            pltpu.VMEM(share, BF16),
            pltpu.VMEM((stripes, max(sub, PAD), width), BF16),
            pltpu.VMEM((reps, chunk, width), BF16),
            pltpu.VMEM((reps * edge, stripes * edge), BF16),
            pltpu.VMEM((stripes * edge, reps * edge), BF16),
        ]
        + by_stripe + by_rep + by_rep + by_rep + by_stripe
        + by_rep + by_stripe + by_stripe + by_rep,
        compiler_params=pltpu.CompilerParams(
            collective_id=0, has_side_effects=True, vmem_limit_bytes=48 * 2**20
        ),
    )(tile_row, tile_src, features, tiles, self_weight, neigh_weight, bias.reshape(1, width), cotangent)
    return output, grad_input, grad_self, grad_neigh, grad_bias.reshape(width)


def solution(mesh):
    return jax.shard_map(
        shards,
        mesh=mesh,
        in_specs=(
            P(("island", "stripe", "rep"), None),
            P(("island", "stripe"), "rep", None, None, None),
            P(("island", "stripe"), "rep", None),
            P(("island", "stripe"), "rep", None),
            P(),
            P(),
            P(),
            P(("island", "stripe", "rep"), None),
        ),
        out_specs=(
            P(("island", "stripe", "rep"), None),
            P(("island", "stripe", "rep"), None),
            P("island", None),
            P("island", None),
            P("island"),
        ),
        check_vma=False,
    )
```

```python
import functools

import jax
import jax.numpy as jnp
from jax import lax
from jax.experimental import pallas as pl
from jax.experimental.pallas import tpu as pltpu
from jax.sharding import PartitionSpec as P

MESH = pl.DeviceIdType.MESH
BF16 = jnp.bfloat16
F32 = jnp.float32
PAD = 16
HALVES = 2


def matmul(a, b):
    return jnp.dot(a, b, preferred_element_type=F32)


def matmul_t(a, b):
    return lax.dot_general(a, b, (((1,), (1,)), ((), ())), preferred_element_type=F32)


def send(src, dst, sems, slot, device):
    return pltpu.make_async_remote_copy(
        src_ref=src,
        dst_ref=dst,
        send_sem=sems[0].at[slot],
        recv_sem=sems[1].at[slot],
        device_id=device,
        device_id_type=MESH,
    )


def kernel(
    stripes, reps, sub,
    row_hbm, src_hbm, feat_hbm, tiles_hbm, self_hbm, neigh_hbm, bias_hbm, cot_hbm,
    out_hbm, gin_hbm, all_hbm, gbias_hbm,
    row_ref, src_ref, feat_ref, tiles_ref, self_ref, neigh_ref, bias_ref, cot_ref, load_sem,
    out_ref, gin_ref, all_rep, gbias_ref, store_sem,
    feat_buf, deg_send, deg_buf, agg_send, agg_buf, pull_buf, term_send, term_buf,
    rep_send, rep_buf, str_send, str_buf, adj, adj_t,
    feat_s, feat_r, deg_s, deg_r, agg_s, agg_r, pull_s, pull_r, term_s, term_r,
    rep_s, rep_r, str_s, str_r, gst_s, gst_r, grp_s, grp_r,
):
    island = lax.axis_index("island")
    s = lax.axis_index("stripe")
    r = lax.axis_index("rep")
    edge, width = feat_ref.shape
    slots = tiles_ref.shape[2]
    half = width // HALVES
    cols = [slice(h * half, (h + 1) * half) for h in range(HALVES)]

    def to_stripe(d):
        return (island, lax.rem(s + d, stripes), r)

    def to_rep(e):
        return (island, s, lax.rem(r + e, reps))

    load_feat, load_tiles, load_row, load_src, load_self, load_neigh, load_bias, load_cot = loads = [
        pltpu.make_async_copy(hbm, ref, load_sem.at[i])
        for i, (hbm, ref) in enumerate(
            (
                (feat_hbm, feat_ref),
                (tiles_hbm, tiles_ref),
                (row_hbm, row_ref),
                (src_hbm, src_ref),
                (self_hbm, self_ref),
                (neigh_hbm, neigh_ref),
                (bias_hbm, bias_ref),
                (cot_hbm, cot_ref),
            )
        )
    ]
    store_out, store_gin, store_all, store_gbias = stores = [
        pltpu.make_async_copy(ref, hbm, store_sem.at[i])
        for i, (ref, hbm) in enumerate(
            ((out_ref, out_hbm), (gin_ref, gin_hbm), (all_rep, all_hbm), (gbias_ref, gbias_hbm))
        )
    ]
    pending = []

    barrier = pltpu.get_barrier_semaphore()
    for d in range(1, stripes):
        pl.semaphore_signal(barrier, inc=1, device_id=to_stripe(d), device_id_type=MESH)
    for e in range(1, reps):
        pl.semaphore_signal(barrier, inc=1, device_id=to_rep(e), device_id_type=MESH)
    for load in loads:
        load.start()
    load_feat.wait()
    pl.semaphore_wait(barrier, stripes + reps - 2)

    feat_copies = [
        [
            send(
                feat_ref.at[:, c], feat_buf.at[d, :, c], (feat_s, feat_r), (d, h), to_stripe(d)
            )
            for d in range(1, stripes)
        ]
        for h, c in enumerate(cols)
    ]
    for copies in feat_copies:
        for copy in copies:
            copy.start()
        pending += copies

    for load in (load_tiles, load_row, load_src):
        load.wait()
    tile = [tiles_ref[0, 0, k] for k in range(slots)]
    row = [row_ref[0, 0, k] for k in range(slots)]
    src = [src_ref[0, 0, k] for k in range(slots)]
    ones = jnp.ones((edge, edge), BF16)
    sums = [matmul(t, ones) for t in tile]
    for e in range(reps):
        q = lax.rem(r + e, reps)
        total = jnp.zeros((edge, edge), F32)
        for k in range(slots):
            total = total + jnp.where(row[k] == q, sums[k], 0.0)
        deg_send[e] = total.astype(BF16)
    deg_copies = [
        send(deg_send.at[e], deg_buf.at[e], (deg_s, deg_r), e, to_rep(e)) for e in range(1, reps)
    ]
    for copy in deg_copies:
        copy.start()
    pending += deg_copies

    zero = jnp.zeros((edge, edge), F32)
    tile_f = [t.astype(F32) for t in tile]
    tile_tf = [t.T for t in tile_f]

    def place(ref, e, d, values, q, t):
        total = zero
        for k in range(slots):
            total = total + jnp.where((row[k] == q) & (src[k] == t), values[k], 0.0)
        ref[e * edge:(e + 1) * edge, d * edge:(d + 1) * edge] = total.astype(BF16)

    for d in range(stripes):
        for e in range(reps):
            place(adj, e, d, tile_f, lax.rem(r + e, reps), lax.rem(s + stripes - d, stripes))
    for d in range(stripes):
        for e in range(reps):
            place(adj_t, d, e, tile_tf, lax.rem(r + reps - e, reps), lax.rem(s + d, stripes))

    load_self.wait()
    load_bias.wait()
    load_neigh.wait()
    load_cot.wait()
    feats = feat_ref[...]
    feats_t = feats.astype(F32).T.astype(BF16)
    feat_buf[0] = feats
    pre = matmul(feats, self_ref[...]) + bias_ref[...].reshape(1, width).astype(F32)
    degree = 1.0 + deg_send[0].astype(F32)
    for copy in deg_copies:
        copy.wait_recv()
    for e in range(1, reps):
        degree = degree + deg_buf[e].astype(F32)
    inverse = jnp.concatenate([1.0 / degree] * (width // edge), axis=1)

    agg_copies = []
    agg = []
    for h, c in enumerate(cols):
        for copy in feat_copies[h]:
            copy.wait_recv()
        feat_all = feat_buf[:, :, c].reshape(stripes * edge, half)
        partial = matmul(adj[...], feat_all)
        agg_copies.append([])
        for e in range(1, reps):
            agg_send[e, :, c] = partial[e * edge:(e + 1) * edge].astype(BF16)
            copy = send(
                agg_send.at[e, :, c], agg_buf.at[e, :, c], (agg_s, agg_r), (e, h), to_rep(e)
            )
            copy.start()
            agg_copies[h].append(copy)
        pending += agg_copies[h]
        agg.append(partial[:edge])
    neigh = []
    for h, c in enumerate(cols):
        for copy in agg_copies[h]:
            copy.wait_recv()
        for e in range(1, reps):
            agg[h] = agg[h] + agg_buf[e, :, c].astype(F32)
        neigh.append((agg[h] * inverse[:, c]).astype(BF16))
        pre = pre + matmul(neigh[h], neigh_ref[c, :])
    sigma = jax.nn.sigmoid(pre)
    slope = (cot_ref[...].astype(F32) * sigma * (1.0 + pre * (1.0 - sigma))).astype(BF16)

    chunk = rep_send.shape[1] - PAD
    grad_bias = jnp.sum(slope.astype(F32), axis=0, keepdims=True)
    bias_rows = jnp.broadcast_to(grad_bias, (PAD, width)).astype(BF16)
    lhs = [feats_t] + [n.astype(F32).T.astype(BF16) for n in neigh]
    grads = jnp.concatenate([matmul(a, slope) for a in lhs], axis=0).astype(BF16)
    for c in range(reps):
        rep_send[c, :chunk] = grads[c * chunk:(c + 1) * chunk]
        rep_send[c, chunk:] = bias_rows
    rep_copies = [
        send(
            rep_send.at[lax.rem(r + e, reps)], rep_buf.at[e], (rep_s, rep_r), e, to_rep(e)
        )
        for e in range(1, reps)
    ]
    for copy in rep_copies:
        copy.start()
    pending += rep_copies

    pull_copies = []
    for h, c in enumerate(cols):
        pull_buf[0, :, c] = (matmul_t(slope, neigh_ref[c, :]) * inverse[:, c]).astype(BF16)
        pull_copies.append(
            [
                send(
                    pull_buf.at[0, :, c], pull_buf.at[e, :, c], (pull_s, pull_r), (e, h), to_rep(e)
                )
                for e in range(1, reps)
            ]
        )
        for copy in pull_copies[h]:
            copy.start()
        pending += pull_copies[h]
    out_ref[...] = (pre * sigma).astype(BF16)
    store_out.start()
    grad_input = matmul_t(slope, self_ref[...])

    term_copies = []
    own_term = []

    def terms(h, c):
        for copy in pull_copies[h]:
            copy.wait_recv()
        pull_all = pull_buf[:, :, c].reshape(reps * edge, half)
        term = matmul(adj_t[...], pull_all).astype(BF16)
        for d in range(1, stripes):
            term_send[d, :, c] = term[d * edge:(d + 1) * edge]
            copy = send(
                term_send.at[d, :, c], term_buf.at[d, :, c], (term_s, term_r), (d, h), to_stripe(d)
            )
            copy.start()
            term_copies.append(copy)
            pending.append(copy)
        own_term.append(term[:edge].astype(F32))

    share = rep_send[r].astype(F32)
    for copy in rep_copies:
        copy.wait_recv()
    for e in range(1, reps):
        share = share + rep_buf[e].astype(F32)
    share = share.astype(BF16)
    if sub:
        for c in range(stripes):
            str_send[c, :sub] = share[c * sub:(c + 1) * sub]
            str_send[c, sub:] = share[chunk:]
        str_copies = [
            send(
                str_send.at[lax.rem(s + d, stripes)], str_buf.at[d], (str_s, str_r), d, to_stripe(d)
            )
            for d in range(1, stripes)
        ]
        part = str_send[s].astype(F32)
    else:
        str_send[0] = share
        str_copies = [
            send(str_send.at[0], str_buf.at[d], (str_s, str_r), d, to_stripe(d))
            for d in range(1, stripes)
        ]
        part = share.astype(F32)
    for copy in str_copies:
        copy.start()
    pending += str_copies
    for h in range(HALVES - 1):
        terms(h, cols[h])
    for copy in str_copies:
        copy.wait_recv()
    for d in range(1, stripes):
        part = part + str_buf[d].astype(F32)
    rows = sub if sub else chunk
    gbias_ref[...] = part[rows]
    store_gbias.start()
    grp_copies = []

    def forward(t):
        for e in range(1, reps):
            share_rows = all_rep.at[r, pl.ds(t * rows, rows)]
            copy = send(
                share_rows, share_rows, (grp_s, grp_r), (e, t if sub else 0), to_rep(e)
            )
            copy.start()
            grp_copies.append(copy)
            pending.append(copy)

    if sub:
        all_rep[r, pl.ds(pl.multiple_of(s * rows, rows), rows)] = part[:rows].astype(BF16)
        gst_copies = [
            send(
                all_rep.at[r, pl.ds(pl.multiple_of(s * rows, rows), rows)],
                all_rep.at[r, pl.ds(pl.multiple_of(s * rows, rows), rows)],
                (gst_s, gst_r), d, to_stripe(d),
            )
            for d in range(1, stripes)
        ]
        for copy in gst_copies:
            copy.start()
        pending += gst_copies
        forward(s)
        terms(HALVES - 1, cols[HALVES - 1])
        for d, copy in enumerate(gst_copies, 1):
            copy.wait_recv()
            forward(lax.rem(s + stripes - d, stripes))
    else:
        all_rep[r] = part[:rows].astype(BF16)
        forward(0)
        terms(HALVES - 1, cols[HALVES - 1])

    grad_input = grad_input + jnp.concatenate(own_term, axis=1)
    for copy in term_copies:
        copy.wait_recv()
    for d in range(1, stripes):
        grad_input = grad_input + term_buf[d].astype(F32)
    gin_ref[...] = grad_input
    store_gin.start()

    for copy in grp_copies:
        copy.wait_recv()
    store_all.start()
    for copy in pending:
        copy.wait_send()
    for store in stores:
        store.wait()


def finish(
    out_in, gin_in, all_in, gbias_in, out_hbm, gin_hbm, gself_hbm, gneigh_hbm, gbias_hbm,
    out_ref, gin_ref, all_ref, gbias_ref, gself_ref, gneigh_ref, load_sem, store_sem,
):
    loads = [
        pltpu.make_async_copy(hbm, ref, load_sem.at[i])
        for i, (hbm, ref) in enumerate(
            ((all_in, all_ref), (gin_in, gin_ref), (out_in, out_ref), (gbias_in, gbias_ref))
        )
    ]
    stores = [
        pltpu.make_async_copy(ref, hbm, store_sem.at[i])
        for i, (ref, hbm) in enumerate(
            (
                (gself_ref, gself_hbm),
                (gneigh_ref, gneigh_hbm),
                (gin_ref, gin_hbm),
                (out_ref, out_hbm),
                (gbias_ref, gbias_hbm),
            )
        )
    ]
    for load in loads:
        load.start()
    for load in loads:
        load.wait()
    for store in stores[2:]:
        store.start()
    middle = all_ref.shape[0] // 2
    gself_ref[...] = all_ref[:middle].reshape(gself_ref.shape).astype(F32)
    stores[0].start()
    gneigh_ref[...] = all_ref[middle:].reshape(gneigh_ref.shape).astype(F32)
    stores[1].start()
    for store in stores:
        store.wait()


def shards(features, tiles, tile_row, tile_src, self_weight, neigh_weight, bias, cotangent):
    stripes = lax.axis_size("stripe")
    reps = lax.axis_size("rep")
    edge, width = features.shape
    chunk = 2 * self_weight.shape[0] // reps
    sub = chunk // stripes if chunk % (PAD * stripes) == 0 else 0
    share = (stripes, sub + PAD, width) if sub else (stripes, chunk + PAD, width)
    hbm = pl.BlockSpec(memory_space=pl.ANY)
    dma = pltpu.SemaphoreType.DMA
    by_rep = [dma((reps,)), dma((reps,))]
    by_stripe = [dma((stripes,)), dma((stripes,))]
    by_rep_half = [dma((reps, HALVES)), dma((reps, HALVES))]
    by_stripe_half = [dma((stripes, HALVES)), dma((stripes, HALVES))]
    by_rep_stripe = [dma((reps, stripes)), dma((reps, stripes))]
    out_shape = (
        jax.ShapeDtypeStruct((edge, width), BF16),
        jax.ShapeDtypeStruct((edge, width), F32),
        jax.ShapeDtypeStruct(self_weight.shape, F32),
        jax.ShapeDtypeStruct(neigh_weight.shape, F32),
        jax.ShapeDtypeStruct((width,), F32),
    )
    shares = jax.ShapeDtypeStruct((reps, chunk, width), BF16)
    staged = (out_shape[0], out_shape[1], shares, out_shape[4])
    results = pl.pallas_call(
        functools.partial(kernel, stripes, reps, sub),
        out_shape=staged,
        in_specs=[hbm] * 8,
        out_specs=(hbm,) * 4,
        scratch_shapes=[
            pltpu.SMEM(tile_row.shape, jnp.int32),
            pltpu.SMEM(tile_src.shape, jnp.int32),
            pltpu.VMEM(features.shape, BF16),
            pltpu.VMEM(tiles.shape, BF16),
            pltpu.VMEM(self_weight.shape, BF16),
            pltpu.VMEM(neigh_weight.shape, BF16),
            pltpu.VMEM(bias.shape, BF16),
            pltpu.VMEM(cotangent.shape, BF16),
            dma((8,)),
            *(pltpu.VMEM(out.shape, out.dtype) for out in staged),
            dma((4,)),
            pltpu.VMEM((stripes, edge, width), BF16),
            pltpu.VMEM((reps, edge, edge), BF16),
            pltpu.VMEM((reps, edge, edge), BF16),
            pltpu.VMEM((reps, edge, width), BF16),
            pltpu.VMEM((reps, edge, width), BF16),
            pltpu.VMEM((reps, edge, width), BF16),
            pltpu.VMEM((stripes, edge, width), BF16),
            pltpu.VMEM((stripes, edge, width), BF16),
            pltpu.VMEM((reps, chunk + PAD, width), BF16),
            pltpu.VMEM((reps, chunk + PAD, width), BF16),
            pltpu.VMEM(share, BF16),
            pltpu.VMEM(share, BF16),
            pltpu.VMEM((reps * edge, stripes * edge), BF16),
            pltpu.VMEM((stripes * edge, reps * edge), BF16),
        ]
        + by_stripe_half + by_rep + by_rep_half + by_rep_half + by_stripe_half
        + by_rep + by_stripe + by_stripe + by_rep_stripe,
        compiler_params=pltpu.CompilerParams(
            collective_id=0, has_side_effects=True, vmem_limit_bytes=60 * 2**20
        ),
    )(tile_row, tile_src, features, tiles, self_weight, neigh_weight, bias, cotangent)
    return pl.pallas_call(
        finish,
        out_shape=out_shape,
        in_specs=[hbm] * 4,
        out_specs=(hbm,) * 5,
        scratch_shapes=[
            *(pltpu.VMEM(out.shape, out.dtype) for out in staged + out_shape[2:4]),
            dma((4,)),
            dma((5,)),
        ],
        compiler_params=pltpu.CompilerParams(vmem_limit_bytes=60 * 2**20),
    )(*results)


def solution(mesh):
    return jax.shard_map(
        shards,
        mesh=mesh,
        in_specs=(
            P(("island", "stripe", "rep"), None),
            P(("island", "stripe"), "rep", None, None, None),
            P(("island", "stripe"), "rep", None),
            P(("island", "stripe"), "rep", None),
            P(),
            P(),
            P(),
            P(("island", "stripe", "rep"), None),
        ),
        out_specs=(
            P(("island", "stripe", "rep"), None),
            P(("island", "stripe", "rep"), None),
            P("island", None),
            P("island", None),
            P("island"),
        ),
        check_vma=False,
    )
```

```python
import functools

import jax
import jax.numpy as jnp
from jax import lax
from jax.experimental import pallas as pl
from jax.experimental.pallas import tpu as pltpu
from jax.sharding import PartitionSpec as P

MESH = pl.DeviceIdType.MESH
BF16 = jnp.bfloat16
F32 = jnp.float32
PAD = 16
HALVES = 2
CORES = 2


def matmul(a, b):
    return jnp.dot(a, b, preferred_element_type=F32)


def matmul_t(a, b):
    return lax.dot_general(a, b, (((1,), (1,)), ((), ())), preferred_element_type=F32)


def send(src, dst, sems, slot, device):
    return pltpu.make_async_remote_copy(
        src_ref=src,
        dst_ref=dst,
        send_sem=sems[0].at[slot],
        recv_sem=sems[1].at[slot],
        device_id=device,
        device_id_type=MESH,
    )


def kernel(
    stripes, reps, owners,
    row_hbm, src_hbm, feat_hbm, tiles_hbm, self_hbm, neigh_hbm, bias_hbm, cot_hbm,
    out_hbm, gin_hbm, all_hbm, gbias_hbm,
    row_ref, src_ref, feat_ref, tiles_ref, self_ref, neigh_ref, bias_ref, cot_ref, load_sem,
    out_ref, gin_ref, all_rep, gbias_ref, store_sem,
    feat_buf, deg_send, deg_buf, agg_send, agg_buf, pull_buf, term_send, term_buf,
    grads, core_buf, chip_send, chip_buf, adj, adj_t,
    feat_s, feat_r, deg_s, deg_r, agg_s, agg_r, pull_s, pull_r, term_s, term_r,
    core_s, core_r, chip_s, chip_r, all_s, all_r, pair_s, pair_r,
):
    island = lax.axis_index("island")
    s = lax.axis_index("stripe")
    r = lax.axis_index("rep")
    edge, width = feat_ref.shape
    slots = tiles_ref.shape[2]
    half = width // HALVES
    cols = [slice(h * half, (h + 1) * half) for h in range(HALVES)]

    def to_stripe(d):
        return (island, lax.rem(s + d, stripes), r)

    def to_rep(e):
        return (island, s, lax.rem(r + e, reps))

    load_feat, load_tiles, load_row, load_src, load_self, load_neigh, load_bias, load_cot = loads = [
        pltpu.make_async_copy(hbm, ref, load_sem.at[i])
        for i, (hbm, ref) in enumerate(
            (
                (feat_hbm, feat_ref),
                (tiles_hbm, tiles_ref),
                (row_hbm, row_ref),
                (src_hbm, src_ref),
                (self_hbm, self_ref),
                (neigh_hbm, neigh_ref),
                (bias_hbm, bias_ref),
                (cot_hbm, cot_ref),
            )
        )
    ]
    store_out, store_gin, store_all, store_gbias = stores = [
        pltpu.make_async_copy(ref, hbm, store_sem.at[i])
        for i, (ref, hbm) in enumerate(
            ((out_ref, out_hbm), (gin_ref, gin_hbm), (all_rep, all_hbm), (gbias_ref, gbias_hbm))
        )
    ]
    pending = []

    core = lax.rem(r, CORES)
    chips = reps // CORES
    others = [(d, x) for d in range(stripes) for x in range(chips)][1:]

    def chip_at(d, x):
        return lax.rem(s + d, stripes), lax.rem(r // CORES + x, chips)

    def to_chip(d, x):
        stripe, chip = chip_at(d, x)
        return (island, stripe, chip * CORES + core)

    def number(d, x):
        stripe, chip = chip_at(d, x)
        return stripe * chips + chip

    partner = (island, s, r + 1 - 2 * core)

    barrier = pltpu.get_barrier_semaphore()
    greeted = [to_chip(d, x) for d, x in others] + [to_rep(e) for e in range(1, reps, 2)]
    for device in greeted:
        pl.semaphore_signal(barrier, inc=1, device_id=device, device_id_type=MESH)
    for load in loads:
        load.start()
    load_feat.wait()
    pl.semaphore_wait(barrier, len(greeted))

    feat_copies = [
        [
            send(
                feat_ref.at[:, c], feat_buf.at[d, :, c], (feat_s, feat_r), (d, h), to_stripe(d)
            )
            for d in range(1, stripes)
        ]
        for h, c in enumerate(cols)
    ]
    for copies in feat_copies:
        for copy in copies:
            copy.start()
        pending += copies

    for load in (load_tiles, load_row, load_src):
        load.wait()
    tile = [tiles_ref[0, 0, k] for k in range(slots)]
    row = [row_ref[0, 0, k] for k in range(slots)]
    src = [src_ref[0, 0, k] for k in range(slots)]
    ones = jnp.ones((edge, edge), BF16)
    sums = [matmul(t, ones) for t in tile]
    for e in range(reps):
        q = lax.rem(r + e, reps)
        total = jnp.zeros((edge, edge), F32)
        for k in range(slots):
            total = total + jnp.where(row[k] == q, sums[k], 0.0)
        deg_send[e] = total.astype(BF16)
    deg_copies = [
        send(deg_send.at[e], deg_buf.at[e], (deg_s, deg_r), e, to_rep(e)) for e in range(1, reps)
    ]
    for copy in deg_copies:
        copy.start()
    pending += deg_copies

    zero = jnp.zeros((edge, edge), F32)
    tile_f = [t.astype(F32) for t in tile]
    tile_tf = [t.T for t in tile_f]

    def place(ref, e, d, values, q, t):
        total = zero
        for k in range(slots):
            total = total + jnp.where((row[k] == q) & (src[k] == t), values[k], 0.0)
        ref[e * edge:(e + 1) * edge, d * edge:(d + 1) * edge] = total.astype(BF16)

    for d in range(stripes):
        for e in range(reps):
            place(adj, e, d, tile_f, lax.rem(r + e, reps), lax.rem(s + stripes - d, stripes))
    for d in range(stripes):
        for e in range(reps):
            place(adj_t, d, e, tile_tf, lax.rem(r + reps - e, reps), lax.rem(s + d, stripes))

    load_self.wait()
    load_bias.wait()
    load_neigh.wait()
    load_cot.wait()
    feats = feat_ref[...]
    feats_t = feats.astype(F32).T.astype(BF16)
    feat_buf[0] = feats
    pre = matmul(feats, self_ref[...]) + bias_ref[...].reshape(1, width).astype(F32)
    degree = 1.0 + deg_send[0].astype(F32)
    for copy in deg_copies:
        copy.wait_recv()
    for e in range(1, reps):
        degree = degree + deg_buf[e].astype(F32)
    inverse = jnp.concatenate([1.0 / degree] * (width // edge), axis=1)

    agg_copies = []
    agg = []
    for h, c in enumerate(cols):
        for copy in feat_copies[h]:
            copy.wait_recv()
        feat_all = feat_buf[:, :, c].reshape(stripes * edge, half)
        partial = matmul(adj[...], feat_all)
        agg_copies.append([])
        for e in range(1, reps):
            agg_send[e, :, c] = partial[e * edge:(e + 1) * edge].astype(BF16)
            copy = send(
                agg_send.at[e, :, c], agg_buf.at[e, :, c], (agg_s, agg_r), (e, h), to_rep(e)
            )
            copy.start()
            agg_copies[h].append(copy)
        pending += agg_copies[h]
        agg.append(partial[:edge])
    neigh = []
    for h, c in enumerate(cols):
        for copy in agg_copies[h]:
            copy.wait_recv()
        for e in range(1, reps):
            agg[h] = agg[h] + agg_buf[e, :, c].astype(F32)
        neigh.append((agg[h] * inverse[:, c]).astype(BF16))
        pre = pre + matmul(neigh[h], neigh_ref[c, :])
    sigma = jax.nn.sigmoid(pre)
    slope = (cot_ref[...].astype(F32) * sigma * (1.0 + pre * (1.0 - sigma))).astype(BF16)

    grads[0] = matmul(feats_t, slope).astype(BF16)
    neigh_t = jnp.concatenate([n.astype(F32).T.astype(BF16) for n in neigh], axis=0)
    grads[1] = matmul(neigh_t, slope).astype(BF16)
    core_copy = send(grads.at[1 - core], core_buf, (core_s, core_r), 0, partner)
    core_copy.start()
    pending.append(core_copy)
    grad_bias = jnp.sum(slope.astype(F32), axis=0, keepdims=True)
    pull_buf[0, edge:] = jnp.broadcast_to(grad_bias, (PAD, width)).astype(BF16)

    pull_copies = []
    for h, c in enumerate(cols):
        pull_buf[0, :edge, c] = (matmul_t(slope, neigh_ref[c, :]) * inverse[:, c]).astype(BF16)
        pull_copies.append(
            [
                send(
                    pull_buf.at[0, :, c], pull_buf.at[e, :, c], (pull_s, pull_r), (e, h), to_rep(e)
                )
                for e in range(1, reps)
            ]
        )
        for copy in pull_copies[h]:
            copy.start()
        pending += pull_copies[h]

    rows = grads.shape[1] // owners
    me = number(0, 0)

    def when(index, step):
        if owners == stripes * chips:
            step()
        else:
            pl.when(index < owners)(step)

    def share_of(ref, index):
        return ref.at[pl.ds(pl.multiple_of(index * rows, rows), rows)]

    core_copy.wait_recv()
    chip_send[...] = (grads[core].astype(F32) + core_buf[...].astype(F32)).astype(BF16)
    chip_copies = [
        send(
            share_of(chip_send, lax.rem(number(d, x), owners)), chip_buf.at[n],
            (chip_s, chip_r), n, to_chip(d, x),
        )
        for n, (d, x) in enumerate(others)
    ]
    for (d, x), copy in zip(others, chip_copies):
        when(number(d, x), copy.start)

    out_ref[...] = (pre * sigma).astype(BF16)
    store_out.start()
    grad_input = matmul_t(slope, self_ref[...])

    term_copies = []
    own_term = []
    own_bias = []

    def terms(h, c):
        for copy in pull_copies[h]:
            copy.wait_recv()
        pull_all = pull_buf[:, :edge, c].reshape(reps * edge, half)
        bias_sum = grad_bias[:, c]
        for e in range(1, reps):
            bias_sum = bias_sum + pull_buf[e, edge:, c].astype(F32)[:1]
        own_bias.append(bias_sum)
        bias_rows = jnp.broadcast_to(bias_sum, (PAD, half)).astype(BF16)
        term = matmul(adj_t[...], pull_all).astype(BF16)
        for d in range(1, stripes):
            term_send[d, edge:, c] = bias_rows
            term_send[d, :edge, c] = term[d * edge:(d + 1) * edge]
            copy = send(
                term_send.at[d, :, c], term_buf.at[d, :, c], (term_s, term_r), (d, h), to_stripe(d)
            )
            copy.start()
            term_copies.append(copy)
            pending.append(copy)
        own_term.append(term[:edge].astype(F32))

    for h in range(HALVES - 1):
        terms(h, cols[h])

    def total():
        part = share_of(chip_send, me)[...].astype(F32)
        for n, copy in enumerate(chip_copies):
            copy.wait_recv()
            part = part + chip_buf[n].astype(F32)
        mine = share_of(all_rep.at[core], me)
        mine[...] = part.astype(BF16)
        for copy in all_copies:
            copy.start()

    def spread_share(index, n):
        rows_ref = share_of(all_rep.at[core], lax.rem(index, owners))
        return send(rows_ref, rows_ref, (pair_s, pair_r), n, partner)

    mine = share_of(all_rep.at[core], lax.rem(me, owners))
    all_copies = [
        send(mine, mine, (all_s, all_r), n, to_chip(d, x)) for n, (d, x) in enumerate(others)
    ]
    when(me, total)
    pair_copies = [(me, spread_share(me, len(others)))]
    when(me, pair_copies[0][1].start)
    terms(HALVES - 1, cols[HALVES - 1])
    for n, (d, x) in enumerate(others):
        index = number(stripes - d, chips - x)
        when(index, all_copies[n].wait_recv)
        copy = spread_share(index, n)
        when(index, copy.start)
        pair_copies.append((index, copy))

    grad_input = grad_input + jnp.concatenate(own_term, axis=1)
    for copy in term_copies:
        copy.wait_recv()
    for d in range(1, stripes):
        grad_input = grad_input + term_buf[d, :edge].astype(F32)
    bias_sum = jnp.concatenate(own_bias, axis=1)
    for d in range(1, stripes):
        bias_sum = bias_sum + term_buf[d, edge:].astype(F32)[:1]
    gbias_ref[...] = bias_sum[0]
    store_gbias.start()
    gin_ref[...] = grad_input
    store_gin.start()

    for index, copy in pair_copies:
        when(index, copy.wait_recv)
    store_all.start()
    for (d, x), copy in zip(others, chip_copies):
        when(number(d, x), copy.wait_send)
    for copy in all_copies:
        when(me, copy.wait_send)
    for index, copy in pair_copies:
        when(index, copy.wait_send)
    for copy in pending:
        copy.wait_send()
    for store in stores:
        store.wait()


def finish(
    out_in, gin_in, all_in, gbias_in, out_hbm, gin_hbm, gself_hbm, gneigh_hbm, gbias_hbm,
    out_ref, gin_ref, all_ref, gbias_ref, gself_ref, gneigh_ref, load_sem, store_sem,
):
    loads = [
        pltpu.make_async_copy(hbm, ref, load_sem.at[i])
        for i, (hbm, ref) in enumerate(
            ((all_in, all_ref), (gin_in, gin_ref), (out_in, out_ref), (gbias_in, gbias_ref))
        )
    ]
    stores = [
        pltpu.make_async_copy(ref, hbm, store_sem.at[i])
        for i, (ref, hbm) in enumerate(
            (
                (gself_ref, gself_hbm),
                (gneigh_ref, gneigh_hbm),
                (gin_ref, gin_hbm),
                (out_ref, out_hbm),
                (gbias_ref, gbias_hbm),
            )
        )
    ]
    for load in loads:
        load.start()
    for load in loads:
        load.wait()
    for store in stores[2:]:
        store.start()
    gself_ref[...] = all_ref[0].astype(F32)
    stores[0].start()
    gneigh_ref[...] = all_ref[1].astype(F32)
    stores[1].start()
    for store in stores:
        store.wait()


def shards(features, tiles, tile_row, tile_src, self_weight, neigh_weight, bias, cotangent):
    stripes = lax.axis_size("stripe")
    reps = lax.axis_size("rep")
    edge, width = features.shape
    chips = stripes * reps // CORES
    depth = self_weight.shape[0]
    owners = min(chips, depth // PAD)
    rows = depth // owners
    hbm = pl.BlockSpec(memory_space=pl.ANY)
    dma = pltpu.SemaphoreType.DMA
    by_rep = [dma((reps,)), dma((reps,))]
    by_rep_half = [dma((reps, HALVES)), dma((reps, HALVES))]
    by_stripe_half = [dma((stripes, HALVES)), dma((stripes, HALVES))]
    by_chip = [dma((chips,)), dma((chips,))]
    out_shape = (
        jax.ShapeDtypeStruct((edge, width), BF16),
        jax.ShapeDtypeStruct((edge, width), F32),
        jax.ShapeDtypeStruct(self_weight.shape, F32),
        jax.ShapeDtypeStruct(neigh_weight.shape, F32),
        jax.ShapeDtypeStruct((width,), F32),
    )
    shares = jax.ShapeDtypeStruct((CORES, depth, width), BF16)
    staged = (out_shape[0], out_shape[1], shares, out_shape[4])
    results = pl.pallas_call(
        functools.partial(kernel, stripes, reps, owners),
        out_shape=staged,
        in_specs=[hbm] * 8,
        out_specs=(hbm,) * 4,
        scratch_shapes=[
            pltpu.SMEM(tile_row.shape, jnp.int32),
            pltpu.SMEM(tile_src.shape, jnp.int32),
            pltpu.VMEM(features.shape, BF16),
            pltpu.VMEM(tiles.shape, BF16),
            pltpu.VMEM(self_weight.shape, BF16),
            pltpu.VMEM(neigh_weight.shape, BF16),
            pltpu.VMEM(bias.shape, BF16),
            pltpu.VMEM(cotangent.shape, BF16),
            dma((8,)),
            *(pltpu.VMEM(out.shape, out.dtype) for out in staged),
            dma((4,)),
            pltpu.VMEM((stripes, edge, width), BF16),
            pltpu.VMEM((reps, edge, edge), BF16),
            pltpu.VMEM((reps, edge, edge), BF16),
            pltpu.VMEM((reps, edge, width), BF16),
            pltpu.VMEM((reps, edge, width), BF16),
            pltpu.VMEM((reps, edge + PAD, width), BF16),
            pltpu.VMEM((stripes, edge + PAD, width), BF16),
            pltpu.VMEM((stripes, edge + PAD, width), BF16),
            pltpu.VMEM((CORES, depth, width), BF16),
            pltpu.VMEM((depth, width), BF16),
            pltpu.VMEM((depth, width), BF16),
            pltpu.VMEM((chips, rows, width), BF16),
            pltpu.VMEM((reps * edge, stripes * edge), BF16),
            pltpu.VMEM((stripes * edge, reps * edge), BF16),
        ]
        + by_stripe_half + by_rep + by_rep_half + by_rep_half + by_stripe_half
        + [dma((1,)), dma((1,))] + by_chip + by_chip + by_chip,
        compiler_params=pltpu.CompilerParams(
            collective_id=0, has_side_effects=True, vmem_limit_bytes=60 * 2**20
        ),
    )(tile_row, tile_src, features, tiles, self_weight, neigh_weight, bias, cotangent)
    return pl.pallas_call(
        finish,
        out_shape=out_shape,
        in_specs=[hbm] * 4,
        out_specs=(hbm,) * 5,
        scratch_shapes=[
            *(pltpu.VMEM(out.shape, out.dtype) for out in staged + out_shape[2:4]),
            dma((4,)),
            dma((5,)),
        ],
        compiler_params=pltpu.CompilerParams(vmem_limit_bytes=60 * 2**20),
    )(*results)


def solution(mesh):
    return jax.shard_map(
        shards,
        mesh=mesh,
        in_specs=(
            P(("island", "stripe", "rep"), None),
            P(("island", "stripe"), "rep", None, None, None),
            P(("island", "stripe"), "rep", None),
            P(("island", "stripe"), "rep", None),
            P(),
            P(),
            P(),
            P(("island", "stripe", "rep"), None),
        ),
        out_specs=(
            P(("island", "stripe", "rep"), None),
            P(("island", "stripe", "rep"), None),
            P("island", None),
            P("island", None),
            P("island"),
        ),
        check_vma=False,
    )
```

```python
import functools

import jax
import jax.numpy as jnp
from jax import lax
from jax.experimental import pallas as pl
from jax.experimental.pallas import tpu as pltpu
from jax.sharding import PartitionSpec as P

MESH = pl.DeviceIdType.MESH
BF16 = jnp.bfloat16
F32 = jnp.float32
PAD = 16
HALVES = 2
CORES = 2


def matmul(a, b):
    return jnp.dot(a, b, preferred_element_type=F32)


def matmul_t(a, b):
    return lax.dot_general(a, b, (((1,), (1,)), ((), ())), preferred_element_type=F32)


def send(src, dst, sems, slot, device):
    return pltpu.make_async_remote_copy(
        src_ref=src,
        dst_ref=dst,
        send_sem=sems[0].at[slot],
        recv_sem=sems[1].at[slot],
        device_id=device,
        device_id_type=MESH,
    )


def kernel(
    stripes, reps, owners,
    row_hbm, src_hbm, feat_hbm, tiles_hbm, self_hbm, neigh_hbm, bias_hbm, cot_hbm,
    out_hbm, gin_hbm, all_hbm, gbias_hbm,
    row_ref, src_ref, feat_ref, tiles_ref, self_ref, neigh_ref, bias_ref, cot_ref, load_sem,
    out_ref, gin_ref, all_rep, gbias_ref, store_sem,
    feat_buf, deg_send, deg_buf, agg_send, agg_buf, pull_buf, term_send, term_buf,
    grads, core_buf, chip_send, chip_buf, adj, adj_t,
    feat_s, feat_r, deg_s, deg_r, agg_s, agg_r, pull_s, pull_r, term_s, term_r,
    core_s, core_r, chip_s, chip_r, all_s, all_r, pair_s, pair_r,
):
    island = lax.axis_index("island")
    s = lax.axis_index("stripe")
    r = lax.axis_index("rep")
    edge, width = feat_ref.shape
    slots = tiles_ref.shape[2]
    half = width // HALVES
    cols = [slice(h * half, (h + 1) * half) for h in range(HALVES)]

    def to_stripe(d):
        return (island, lax.rem(s + d, stripes), r)

    def to_rep(e):
        return (island, s, lax.rem(r + e, reps))

    load_feat, load_tiles, load_row, load_src, load_self, load_neigh, load_bias, load_cot = loads = [
        pltpu.make_async_copy(hbm, ref, load_sem.at[i])
        for i, (hbm, ref) in enumerate(
            (
                (feat_hbm, feat_ref),
                (tiles_hbm, tiles_ref),
                (row_hbm, row_ref),
                (src_hbm, src_ref),
                (self_hbm, self_ref),
                (neigh_hbm, neigh_ref),
                (bias_hbm, bias_ref),
                (cot_hbm, cot_ref),
            )
        )
    ]
    store_out, store_gin, store_all, store_gbias = stores = [
        pltpu.make_async_copy(ref, hbm, store_sem.at[i])
        for i, (ref, hbm) in enumerate(
            ((out_ref, out_hbm), (gin_ref, gin_hbm), (all_rep, all_hbm), (gbias_ref, gbias_hbm))
        )
    ]
    pending = []

    for load in loads:
        load.start()

    core = lax.rem(r, CORES)
    chips = reps // CORES
    others = [(d, x) for d in range(stripes) for x in range(chips)][1:]

    def chip_at(d, x):
        return lax.rem(s + d, stripes), lax.rem(r // CORES + x, chips)

    def to_chip(d, x):
        stripe, chip = chip_at(d, x)
        return (island, stripe, chip * CORES + core)

    def number(d, x):
        stripe, chip = chip_at(d, x)
        return stripe * chips + chip

    partner = (island, s, r + 1 - 2 * core)

    barrier = pltpu.get_barrier_semaphore()
    greeted = [to_chip(d, x) for d, x in others] + [to_rep(e) for e in range(1, reps, 2)]
    for device in greeted:
        pl.semaphore_signal(barrier, inc=1, device_id=device, device_id_type=MESH)
    load_feat.wait()
    pl.semaphore_wait(barrier, len(greeted))

    feat_copies = [
        [
            send(
                feat_ref.at[:, c], feat_buf.at[d, :, c], (feat_s, feat_r), (d, h), to_stripe(d)
            )
            for d in range(1, stripes)
        ]
        for h, c in enumerate(cols)
    ]
    for copies in feat_copies:
        for copy in copies:
            copy.start()
        pending += copies

    for load in (load_tiles, load_row, load_src):
        load.wait()
    tile = [tiles_ref[0, 0, k] for k in range(slots)]
    row = [row_ref[0, 0, k] for k in range(slots)]
    src = [src_ref[0, 0, k] for k in range(slots)]
    ones = jnp.ones((edge, edge), BF16)
    sums = [matmul(t, ones) for t in tile]
    for e in range(reps):
        q = lax.rem(r + e, reps)
        total = jnp.zeros((edge, edge), F32)
        for k in range(slots):
            total = total + jnp.where(row[k] == q, sums[k], 0.0)
        deg_send[e] = total.astype(BF16)
    deg_copies = [
        send(deg_send.at[e], deg_buf.at[e], (deg_s, deg_r), e, to_rep(e)) for e in range(1, reps)
    ]
    for copy in deg_copies:
        copy.start()
    pending += deg_copies

    zero = jnp.zeros((edge, edge), F32)
    tile_f = [t.astype(F32) for t in tile]
    tile_tf = [t.T for t in tile_f]

    def place(ref, e, d, values, q, t):
        total = zero
        for k in range(slots):
            total = total + jnp.where((row[k] == q) & (src[k] == t), values[k], 0.0)
        ref[e * edge:(e + 1) * edge, d * edge:(d + 1) * edge] = total.astype(BF16)

    for d in range(stripes):
        for e in range(reps):
            place(adj, e, d, tile_f, lax.rem(r + e, reps), lax.rem(s + stripes - d, stripes))
    for d in range(stripes):
        for e in range(reps):
            place(adj_t, d, e, tile_tf, lax.rem(r + reps - e, reps), lax.rem(s + d, stripes))

    load_self.wait()
    load_bias.wait()
    load_neigh.wait()
    load_cot.wait()
    feats = feat_ref[...]
    feats_t = feats.astype(F32).T.astype(BF16)
    feat_buf[0] = feats
    pre = matmul(feats, self_ref[...]) + bias_ref[...].reshape(1, width).astype(F32)
    degree = 1.0 + deg_send[0].astype(F32)
    for copy in deg_copies:
        copy.wait_recv()
    for e in range(1, reps):
        degree = degree + deg_buf[e].astype(F32)
    inverse = jnp.concatenate([1.0 / degree] * (width // edge), axis=1)

    agg_copies = []
    agg = []
    for h, c in enumerate(cols):
        for copy in feat_copies[h]:
            copy.wait_recv()
        feat_all = feat_buf[:, :, c].reshape(stripes * edge, half)
        partial = matmul(adj[...], feat_all)
        agg_copies.append([])
        for e in range(1, reps):
            agg_send[e, :, c] = partial[e * edge:(e + 1) * edge].astype(BF16)
            copy = send(
                agg_send.at[e, :, c], agg_buf.at[e, :, c], (agg_s, agg_r), (e, h), to_rep(e)
            )
            copy.start()
            agg_copies[h].append(copy)
        pending += agg_copies[h]
        agg.append(partial[:edge])
    neigh = []
    for h, c in enumerate(cols):
        for copy in agg_copies[h]:
            copy.wait_recv()
        for e in range(1, reps):
            agg[h] = agg[h] + agg_buf[e, :, c].astype(F32)
        neigh.append((agg[h] * inverse[:, c]).astype(BF16))
        pre = pre + matmul(neigh[h], neigh_ref[c, :])
    sigma = jax.nn.sigmoid(pre)
    slope = (cot_ref[...].astype(F32) * sigma * (1.0 + pre * (1.0 - sigma))).astype(BF16)

    core_copy = send(grads.at[1 - core], core_buf, (core_s, core_r), 0, partner)

    def weight_grads():
        grads[0] = matmul(feats_t, slope).astype(BF16)
        neigh_t = jnp.concatenate([n.astype(F32).T.astype(BF16) for n in neigh], axis=0)
        grads[1] = matmul(neigh_t, slope).astype(BF16)
        core_copy.start()
        pending.append(core_copy)

    grad_bias = jnp.sum(slope.astype(F32), axis=0, keepdims=True)
    pull_buf[0, edge:] = jnp.broadcast_to(grad_bias, (PAD, width)).astype(BF16)

    pull_copies = []
    for h, c in enumerate(cols):
        pull_buf[0, :edge, c] = (matmul_t(slope, neigh_ref[c, :]) * inverse[:, c]).astype(BF16)
        pull_copies.append(
            [
                send(
                    pull_buf.at[0, :, c], pull_buf.at[e, :, c], (pull_s, pull_r), (e, h), to_rep(e)
                )
                for e in range(1, reps)
            ]
        )
        for copy in pull_copies[h]:
            copy.start()
        pending += pull_copies[h]
        if h == 0:
            weight_grads()

    rows = grads.shape[1] // owners
    me = number(0, 0)

    def when(index, step):
        if owners == stripes * chips:
            step()
        else:
            pl.when(index < owners)(step)

    def share_of(ref, index):
        return ref.at[pl.ds(pl.multiple_of(index * rows, rows), rows)]

    core_copy.wait_recv()
    chip_send[...] = (grads[core].astype(F32) + core_buf[...].astype(F32)).astype(BF16)
    chip_copies = [
        send(
            share_of(chip_send, lax.rem(number(d, x), owners)), chip_buf.at[n],
            (chip_s, chip_r), n, to_chip(d, x),
        )
        for n, (d, x) in enumerate(others)
    ]
    for (d, x), copy in zip(others, chip_copies):
        when(number(d, x), copy.start)

    out_ref[...] = (pre * sigma).astype(BF16)
    store_out.start()
    grad_input = matmul_t(slope, self_ref[...])

    term_copies = []
    own_term = []
    own_bias = []

    def terms(h, c):
        for copy in pull_copies[h]:
            copy.wait_recv()
        pull_all = pull_buf[:, :edge, c].reshape(reps * edge, half)
        bias_sum = grad_bias[:, c]
        for e in range(1, reps):
            bias_sum = bias_sum + pull_buf[e, edge:, c].astype(F32)[:1]
        own_bias.append(bias_sum)
        bias_rows = jnp.broadcast_to(bias_sum, (PAD, half)).astype(BF16)
        term = matmul(adj_t[...], pull_all).astype(BF16)
        for d in range(1, stripes):
            term_send[d, edge:, c] = bias_rows
            term_send[d, :edge, c] = term[d * edge:(d + 1) * edge]
            copy = send(
                term_send.at[d, :, c], term_buf.at[d, :, c], (term_s, term_r), (d, h), to_stripe(d)
            )
            copy.start()
            term_copies.append(copy)
            pending.append(copy)
        own_term.append(term[:edge].astype(F32))

    for h in range(HALVES - 1):
        terms(h, cols[h])

    def total():
        part = share_of(chip_send, me)[...].astype(F32)
        for n, copy in enumerate(chip_copies):
            copy.wait_recv()
            part = part + chip_buf[n].astype(F32)
        mine = share_of(all_rep.at[core], me)
        mine[...] = part.astype(BF16)
        for copy in all_copies:
            copy.start()

    def spread_share(index, n):
        rows_ref = share_of(all_rep.at[core], lax.rem(index, owners))
        return send(rows_ref, rows_ref, (pair_s, pair_r), n, partner)

    mine = share_of(all_rep.at[core], lax.rem(me, owners))
    all_copies = [
        send(mine, mine, (all_s, all_r), n, to_chip(d, x)) for n, (d, x) in enumerate(others)
    ]
    when(me, total)
    pair_copies = [(me, spread_share(me, len(others)))]
    when(me, pair_copies[0][1].start)
    terms(HALVES - 1, cols[HALVES - 1])
    for n, (d, x) in enumerate(others):
        index = number(stripes - d, chips - x)
        when(index, all_copies[n].wait_recv)
        copy = spread_share(index, n)
        when(index, copy.start)
        pair_copies.append((index, copy))

    grad_input = grad_input + jnp.concatenate(own_term, axis=1)
    for copy in term_copies:
        copy.wait_recv()
    for d in range(1, stripes):
        grad_input = grad_input + term_buf[d, :edge].astype(F32)
    bias_sum = jnp.concatenate(own_bias, axis=1)
    for d in range(1, stripes):
        bias_sum = bias_sum + term_buf[d, edge:].astype(F32)[:1]
    gbias_ref[...] = bias_sum[0]
    store_gbias.start()
    gin_ref[...] = grad_input
    store_gin.start()

    for index, copy in pair_copies:
        when(index, copy.wait_recv)
    store_all.start()
    for (d, x), copy in zip(others, chip_copies):
        when(number(d, x), copy.wait_send)
    for copy in all_copies:
        when(me, copy.wait_send)
    for index, copy in pair_copies:
        when(index, copy.wait_send)
    for copy in pending:
        copy.wait_send()
    for store in stores:
        store.wait()


def finish(
    out_in, gin_in, all_in, gbias_in, out_hbm, gin_hbm, gself_hbm, gneigh_hbm, gbias_hbm,
    out_ref, gin_ref, all_ref, gbias_ref, gself_ref, gneigh_ref, load_sem, store_sem,
):
    loads = [
        pltpu.make_async_copy(hbm, ref, load_sem.at[i])
        for i, (hbm, ref) in enumerate(
            ((all_in, all_ref), (gin_in, gin_ref), (out_in, out_ref), (gbias_in, gbias_ref))
        )
    ]
    stores = [
        pltpu.make_async_copy(ref, hbm, store_sem.at[i])
        for i, (ref, hbm) in enumerate(
            (
                (gself_ref, gself_hbm),
                (gneigh_ref, gneigh_hbm),
                (gin_ref, gin_hbm),
                (out_ref, out_hbm),
                (gbias_ref, gbias_hbm),
            )
        )
    ]
    for load in loads:
        load.start()
    for load in loads:
        load.wait()
    for store in stores[2:]:
        store.start()
    gself_ref[...] = all_ref[0].astype(F32)
    stores[0].start()
    gneigh_ref[...] = all_ref[1].astype(F32)
    stores[1].start()
    for store in stores:
        store.wait()


def shards(features, tiles, tile_row, tile_src, self_weight, neigh_weight, bias, cotangent):
    stripes = lax.axis_size("stripe")
    reps = lax.axis_size("rep")
    edge, width = features.shape
    chips = stripes * reps // CORES
    depth = self_weight.shape[0]
    owners = min(chips, depth // PAD)
    rows = depth // owners
    hbm = pl.BlockSpec(memory_space=pl.ANY)
    dma = pltpu.SemaphoreType.DMA
    by_rep = [dma((reps,)), dma((reps,))]
    by_rep_half = [dma((reps, HALVES)), dma((reps, HALVES))]
    by_stripe_half = [dma((stripes, HALVES)), dma((stripes, HALVES))]
    by_chip = [dma((chips,)), dma((chips,))]
    out_shape = (
        jax.ShapeDtypeStruct((edge, width), BF16),
        jax.ShapeDtypeStruct((edge, width), F32),
        jax.ShapeDtypeStruct(self_weight.shape, F32),
        jax.ShapeDtypeStruct(neigh_weight.shape, F32),
        jax.ShapeDtypeStruct((width,), F32),
    )
    shares = jax.ShapeDtypeStruct((CORES, depth, width), BF16)
    staged = (out_shape[0], out_shape[1], shares, out_shape[4])
    results = pl.pallas_call(
        functools.partial(kernel, stripes, reps, owners),
        out_shape=staged,
        in_specs=[hbm] * 8,
        out_specs=(hbm,) * 4,
        scratch_shapes=[
            pltpu.SMEM(tile_row.shape, jnp.int32),
            pltpu.SMEM(tile_src.shape, jnp.int32),
            pltpu.VMEM(features.shape, BF16),
            pltpu.VMEM(tiles.shape, BF16),
            pltpu.VMEM(self_weight.shape, BF16),
            pltpu.VMEM(neigh_weight.shape, BF16),
            pltpu.VMEM(bias.shape, BF16),
            pltpu.VMEM(cotangent.shape, BF16),
            dma((8,)),
            *(pltpu.VMEM(out.shape, out.dtype) for out in staged),
            dma((4,)),
            pltpu.VMEM((stripes, edge, width), BF16),
            pltpu.VMEM((reps, edge, edge), BF16),
            pltpu.VMEM((reps, edge, edge), BF16),
            pltpu.VMEM((reps, edge, width), BF16),
            pltpu.VMEM((reps, edge, width), BF16),
            pltpu.VMEM((reps, edge + PAD, width), BF16),
            pltpu.VMEM((stripes, edge + PAD, width), BF16),
            pltpu.VMEM((stripes, edge + PAD, width), BF16),
            pltpu.VMEM((CORES, depth, width), BF16),
            pltpu.VMEM((depth, width), BF16),
            pltpu.VMEM((depth, width), BF16),
            pltpu.VMEM((chips, rows, width), BF16),
            pltpu.VMEM((reps * edge, stripes * edge), BF16),
            pltpu.VMEM((stripes * edge, reps * edge), BF16),
        ]
        + by_stripe_half + by_rep + by_rep_half + by_rep_half + by_stripe_half
        + [dma((1,)), dma((1,))] + by_chip + by_chip + by_chip,
        compiler_params=pltpu.CompilerParams(
            collective_id=0, has_side_effects=True, vmem_limit_bytes=60 * 2**20
        ),
    )(tile_row, tile_src, features, tiles, self_weight, neigh_weight, bias, cotangent)
    return pl.pallas_call(
        finish,
        out_shape=out_shape,
        in_specs=[hbm] * 4,
        out_specs=(hbm,) * 5,
        scratch_shapes=[
            *(pltpu.VMEM(out.shape, out.dtype) for out in staged + out_shape[2:4]),
            dma((4,)),
            dma((5,)),
        ],
        compiler_params=pltpu.CompilerParams(vmem_limit_bytes=60 * 2**20),
    )(*results)


def solution(mesh):
    return jax.shard_map(
        shards,
        mesh=mesh,
        in_specs=(
            P(("island", "stripe", "rep"), None),
            P(("island", "stripe"), "rep", None, None, None),
            P(("island", "stripe"), "rep", None),
            P(("island", "stripe"), "rep", None),
            P(),
            P(),
            P(),
            P(("island", "stripe", "rep"), None),
        ),
        out_specs=(
            P(("island", "stripe", "rep"), None),
            P(("island", "stripe", "rep"), None),
            P("island", None),
            P("island", None),
            P("island"),
        ),
        check_vma=False,
    )
```
